256 devices in a mesh: row: 16 (over y, x_lo, core), aux: 16 (over z, x_hi).
Axes of the slice: x: 4 (x_hi: 2, x_lo: 2; x = x_hi * 2 + x_lo), y: 4, z: 8, core: 2. Of those that a mesh axis runs over, the one named last changes fastest.
Arguments:
- factors: float32 [16, 6144, 6144], P('aux', 'row'), may hold values from -0.078125 to 0.078125
- orbitals: float32 [6144, 512], P('row'), may hold values from -0.125 to 0.125
Outputs:
- exchange_matrix: float32 [6144, 6144], P(('row', 'aux'))
The draws below stay inside these ranges and needn't reach their ends.
All inputs are finite; a program needn't handle non-finite values.
Results may differ from the reference program's by a relative error of at most 0.00007.
Values sent between devices are 32-bit elements; how exact they have to be, the bound alone decides.
No kernel may reach another device: no remote copies, remote signals or barrier semaphores. Data moves between devices by JAX's collectives and lax.ppermute only.
A program may use at most 64 MiB of HBM per device.

```python
import jax
import jax.numpy as jnp
from jax import lax

NB = 6144
OCC = 512
NAUX = 16


def block_levels(rng, extent, split, smallest, top_value):
    def one(position, parts):
        steps = jax.random.uniform(jax.random.fold_in(jax.random.fold_in(rng, 6), position), (parts,), jnp.float32, smallest / len(split), top_value / len(split))
        return jnp.repeat(jnp.exp(steps), extent[position] // parts).reshape((-1,) + (1,) * (len(extent) - position - 1))

    gain = one(*split[0])
    for cut in split[1:]:
        gain = gain * one(*cut)
    return gain


def gaussian(stream_key, extent, spread, bound, shards=(), kind=jnp.bfloat16):
    level = block_levels(stream_key, extent, shards, -0.22, 0.18) if shards else 1.0
    drawn = jax.random.normal(stream_key, extent, jnp.float32) * spread * level
    return jnp.minimum(jnp.maximum(drawn, -bound), bound).astype(kind)


def setup_inputs(seed: int = 0) -> dict:
    seeds = jax.random.split(jax.random.key(seed), 3)
    factors = gaussian(seeds[0], (NAUX, NB, NB), NB ** -0.5, 0.078125, ((0, 16), (1, 16)), jnp.float32)
    orbitals = gaussian(seeds[1], (NB, OCC), (NAUX * OCC // 4) ** -0.5, 0.125, ((0, 16),), jnp.float32)
    return dict(factors=factors, orbitals=orbitals)


def transform_slab(aux_slab, orbitals):
    return jnp.dot(aux_slab, orbitals, precision=lax.Precision.HIGHEST, preferred_element_type=jnp.float32)


def reference(factors, orbitals):
    half_transformed = lax.map(lambda aux_slab: transform_slab(aux_slab, orbitals), factors)
    flattened = jnp.transpose(half_transformed, (1, 0, 2)).reshape(NB, NAUX * OCC)
    return lax.dot_general(flattened, flattened, (((1,), (1,)), ((), ())), precision=lax.Precision.HIGHEST, preferred_element_type=jnp.float32)
```

```python
import jax
import jax.numpy as jnp
from jax import lax
from jax.sharding import PartitionSpec as P

AXES = ("row", "aux")
NY, NXL, NC, NZ, NXH = 4, 2, 2, 8, 2
CHUNKS = 1


def linear(y, xl, c, z, xh):
    row = ((y % NY) * NXL + xl) * NC + c
    return row * (NZ * NXH) + (z % NZ) * NXH + xh


def move(block, target):
    route = []
    for y in range(NY):
        for xl in range(NXL):
            for c in range(NC):
                for z in range(NZ):
                    for xh in range(NXH):
                        route.append((linear(y, xl, c, z, xh), linear(*target(y, xl, c, z, xh))))
    return lax.ppermute(block, AXES, route)


def swap_cores(b):
    return move(b, lambda y, xl, c, z, xh: (y, xl, 1 - c, z, xh))


def along_y(b, step):
    return move(b, lambda y, xl, c, z, xh: (y + step, xl, c, z, xh))


def along_z(b, step):
    return move(b, lambda y, xl, c, z, xh: (y, xl, c, z + step, xh))


def along_y_by_core(b, sign):
    return move(b, lambda y, xl, c, z, xh: (y + sign * (1 - 2 * c), xl, c, z, xh))


def along_x_by_core(b):
    def target(y, xl, c, z, xh):
        x = (xh * 2 + xl + (1 - 2 * c)) % 4
        return y, x % 2, c, z, x // 2

    return move(b, target)


def flip_x(b, flip_lo, flip_hi):
    return move(b, lambda y, xl, c, z, xh: (y, xl ^ flip_lo, c, z, xh ^ flip_hi))


def mm(a, b):
    return lax.dot_general(
        a, b, (((1,), (0,)), ((), ())), precision=lax.Precision.HIGH, preferred_element_type=jnp.float32
    )


def mm_t(a, b):
    return lax.dot_general(
        a, b, (((1,), (1,)), ((), ())), precision=lax.Precision.HIGH, preferred_element_type=jnp.float32
    )


def reduce_z(s, z):
    def part(d):
        return lax.dynamic_index_in_dim(s, (z + d) % NZ, 1, keepdims=False)

    up = along_z(part(3), 1)
    down = along_z(part(4), -1)
    up = along_z(up + part(2), 1)
    down = along_z(down + part(5), -1)
    up = along_z(up + part(1), 1)
    down = along_z(down + part(6), -1)
    down = along_z(down + part(7), -1)
    return up + down + part(0)


def shards(factors, orbitals):
    block_rows = factors.shape[1]
    occ = orbitals.shape[1]
    half = occ // 2
    width = half // CHUNKS
    row = lax.axis_index("row")
    aux = lax.axis_index("aux")
    y, xl, c = row // 4, (row // 2) % 2, row % 2
    z, xh = aux // 2, aux % 2
    sg = 1 - 2 * c

    f_own = factors[0]
    f_oth = swap_cores(f_own)

    o = orbitals.reshape(block_rows, 2, half)
    mine = lax.dynamic_index_in_dim(o, c, 1, keepdims=False)
    theirs = swap_cores(lax.dynamic_index_in_dim(o, 1 - c, 1, keepdims=False))
    first = jnp.where(c == 0, mine, theirs)
    second = jnp.where(c == 0, theirs, mine)
    piece = jnp.concatenate([first, second], axis=0)

    chip_rows = 2 * block_rows

    def columns(f, yy, ll):
        start = ((yy % NY) * 2 + ll) * chip_rows
        return lax.dynamic_slice(f, (jnp.int32(0), start), (block_rows, chip_rows))

    keep_b, send_b = [], []
    for k in range(CHUNKS):
        v = piece[:, k * width:(k + 1) * width]
        a = along_y_by_core(v, 1)
        x0 = along_x_by_core(v)
        b = along_y_by_core(v, -1)
        x1 = along_x_by_core(a)
        y2 = along_y_by_core(a, 1)
        x2 = along_x_by_core(b)
        y3 = along_y_by_core(x1, 1)
        parts = [
            (v, y, xl), (x0, y, 1 - xl), (a, y - sg, xl), (b, y + sg, xl),
            (x1, y - sg, 1 - xl), (y2, y + 2, xl), (x2, y + sg, 1 - xl), (y3, y + 2, 1 - xl),
        ]
        bk = bs = None
        for block, yy, ll in parts:
            tk = mm(columns(f_own, yy, ll), block)
            ts = mm(columns(f_oth, yy, ll), block)
            bk = tk if bk is None else bk + tk
            bs = ts if bs is None else bs + ts
        keep_b.append(bk)
        send_b.append(bs)

    rk_own, rk_oth, rs_own, rs_oth = [], [], [], []
    cols = {0: [], 1: [], -1: [], 2: []}
    for k in range(CHUNKS):
        bk, bs = keep_b[k], send_b[k]
        both = jnp.concatenate([bk, bs], axis=0)
        n3 = flip_x(both, 0, 1)
        n1 = flip_x(both, 1, 0)
        n2 = flip_x(both, 1, 1)
        own = jnp.concatenate([both, n3], axis=1)
        oth = jnp.concatenate([n1, n2], axis=1)
        rk_own.append(own[:block_rows])
        rs_own.append(own[block_rows:])
        rk_oth.append(oth[:block_rows])
        rs_oth.append(oth[block_rows:])
        mine_c = jnp.where(xh == c, own[:block_rows], own[block_rows:])
        plus = along_y(mine_c, -1)
        minus = along_y(mine_c, 1)
        far = along_y_by_core(jnp.where(c == 0, minus, plus), 1)
        cols[0].append(mine_c)
        cols[1].append(plus)
        cols[-1].append(minus)
        cols[2].append(far)

    r_keep = jnp.concatenate(
        [jnp.concatenate(rk_own, axis=1), jnp.concatenate(rk_oth, axis=1)], axis=0)
    r_send = jnp.concatenate(
        [jnp.concatenate(rs_own, axis=1), jnp.concatenate(rs_oth, axis=1)], axis=0)

    sub = block_rows // NZ

    def reduced(col):
        from_other = swap_cores(mm_t(r_send, col))
        s = mm_t(r_keep, col) + from_other
        return reduce_z(s.reshape(2, NZ, sub, col.shape[0]), z)

    def col(d):
        return jnp.concatenate(cols[d], axis=1)

    k0 = reduced(col(0))
    k1 = reduced(jnp.concatenate([col(1), col(-1)], axis=0))
    k2 = reduced(col(2))
    rel = [k0, k1[..., :block_rows], k2, k1[..., block_rows:]]
    rel = jnp.stack(rel + rel[:3], axis=0)
    ks = lax.dynamic_slice_in_dim(rel, (NY - y) % NY, NY, 0)

    out_rows = sub // 2
    ks = ks.reshape(NY, 2, 2, out_rows, block_rows)
    same = lax.dynamic_index_in_dim(ks, xh, 2, keepdims=False)
    other = lax.dynamic_index_in_dim(ks, 1 - xh, 2, keepdims=False)
    g0 = same[:, 0]
    g1 = flip_x(same[:, 1], 1, 0)
    g2 = flip_x(other[:, 1], 1, 1)
    g3 = flip_x(other[:, 0], 0, 1)
    p00 = jnp.where(xh == 0, g0, g3)
    p01 = jnp.where(xh == 0, g3, g0)
    p10 = jnp.where(xh == 0, g1, g2)
    p11 = jnp.where(xh == 0, g2, g1)
    lo = xl == 0
    blocks = [jnp.where(lo, p00, p10), jnp.where(lo, p01, p11), jnp.where(lo, p10, p00), jnp.where(lo, p11, p01)]
    pieces = [blocks[j][yy] for yy in range(NY) for j in range(4)]
    return jnp.concatenate(pieces, axis=1)


def solution(mesh):
    return jax.shard_map(
        shards,
        mesh=mesh,
        in_specs=(P("aux", "row", None), P("row", None)),
        out_specs=P(("row", "aux"), None),
        check_vma=False,
    )
```

```python
import functools

import jax
import jax.numpy as jnp
from jax import lax
from jax.experimental import pallas as pl
from jax.experimental.pallas import tpu as pltpu
from jax.sharding import PartitionSpec as P

AXES = ("row", "aux")
NY, NXL, NC, NZ, NXH = 4, 2, 2, 8, 2


def linear(y, xl, c, z, xh):
    row = ((y % NY) * NXL + xl) * NC + c
    return row * (NZ * NXH) + (z % NZ) * NXH + xh


def move(block, target):
    route = []
    for y in range(NY):
        for xl in range(NXL):
            for c in range(NC):
                for z in range(NZ):
                    for xh in range(NXH):
                        route.append((linear(y, xl, c, z, xh), linear(*target(y, xl, c, z, xh))))
    return lax.ppermute(block, AXES, route)


def swap_cores(b):
    return move(b, lambda y, xl, c, z, xh: (y, xl, 1 - c, z, xh))


def along_y(b, step):
    return move(b, lambda y, xl, c, z, xh: (y + step, xl, c, z, xh))


def along_z(b, step):
    return move(b, lambda y, xl, c, z, xh: (y, xl, c, z + step, xh))


def along_y_by_core(b, sign):
    return move(b, lambda y, xl, c, z, xh: (y + sign * (1 - 2 * c), xl, c, z, xh))


def along_x_by_core(b):
    def target(y, xl, c, z, xh):
        x = (xh * 2 + xl + (1 - 2 * c)) % 4
        return y, x % 2, c, z, x // 2

    return move(b, target)


def flip_x(b, flip_lo, flip_hi):
    return move(b, lambda y, xl, c, z, xh: (y, xl ^ flip_lo, c, z, xh ^ flip_hi))


def after(value, *earlier):
    return lax.optimization_barrier((value,) + earlier)[0]


def split(v):
    hi = lax.reduce_precision(v, 8, 7)
    return hi.astype(jnp.bfloat16), (v - hi).astype(jnp.bfloat16)


STEPS = 1


def halves(v):
    hi = v.astype(jnp.bfloat16)
    return hi, (v - hi.astype(jnp.float32)).astype(jnp.bfloat16)


def transform_kernel(count, where_ref, own_ref, oth_ref, *refs):
    del where_ref
    c_refs, rest = refs[:count], refs[count:]
    out_ref = rest[-1]
    k = pl.program_id(0)

    @pl.when(k == 0)
    def _():
        out_ref[...] = rest[0][...] if len(rest) == 2 else jnp.zeros_like(out_ref)

    rows, tile = own_ref.shape

    def one(c_ref):
        start = pl.multiple_of(lax.rem(k, STEPS) * tile, tile)
        c_hi, c_lo = halves(c_ref[pl.ds(start, tile), :])
        c_all = jnp.concatenate([c_hi, c_lo, c_hi], axis=0)
        for h, f_ref in enumerate((own_ref, oth_ref)):
            f_hi, f_lo = halves(f_ref[...])
            f_all = jnp.concatenate([f_hi, f_hi, f_lo], axis=1)
            out_ref[h * rows:(h + 1) * rows, :] += jnp.dot(f_all, c_all, preferred_element_type=jnp.float32)

    for p in range(count):
        pl.when(k // STEPS == p)(functools.partial(one, c_refs[p]))


def transform(f_own, f_oth, blocks, indices, acc=None):
    rows = f_own.shape[0]
    depth, width = blocks[0].shape
    count = len(blocks)
    tile = depth // STEPS
    f_spec = pl.BlockSpec((rows, tile), lambda k, w: (0, w[k // STEPS] * STEPS + lax.rem(k, STEPS)))
    whole = pl.BlockSpec((2 * rows, width), lambda k, w: (0, 0))
    extra = [] if acc is None else [acc]
    return pl.pallas_call(
        functools.partial(transform_kernel, count),
        grid_spec=pltpu.PrefetchScalarGridSpec(
            num_scalar_prefetch=1,
            grid=(count * STEPS,),
            in_specs=[f_spec, f_spec] + [whole] * (count + len(extra)),
            out_specs=whole,
        ),
        out_shape=jax.ShapeDtypeStruct((2 * rows, width), jnp.float32),
        input_output_aliases={} if acc is None else {3 + count: 0},
        cost_estimate=pl.CostEstimate(
            flops=12 * count * rows * depth * width, bytes_accessed=12 * count * rows * depth, transcendentals=0),
        compiler_params=pltpu.CompilerParams(vmem_limit_bytes=56 * 1024 * 1024),
    )(jnp.stack(indices).astype(jnp.int32), f_own, f_oth, *blocks, *extra)


def mm_t(a, b):
    return lax.dot_general(a, b, (((1,), (1,)), ((), ())), preferred_element_type=jnp.float32)


def lockstep(*values):
    return lax.optimization_barrier(values)


def reduce_z(part):
    far = part(4)
    h = far.shape[0] // 2
    up, down = along_z(far[:h], 1), along_z(far[h:], -1)
    up, down = lockstep(up, down)
    p, m = part(3), part(5)
    up = jnp.concatenate([p[:h] + up, p[h:]], axis=0)
    down = jnp.concatenate([m[:h], m[h:] + down], axis=0)
    for d in (2, 1):
        up, down = lockstep(along_z(up, 1), along_z(down, -1))
        up, down = up + part(d), down + part(8 - d)
    up, down = lockstep(along_z(up, 1), along_z(down, -1))
    return up + down + part(0)


def shards(factors, orbitals):
    block_rows = factors.shape[1]
    occ = orbitals.shape[1]
    half = occ // 2
    row = lax.axis_index("row")
    aux = lax.axis_index("aux")
    y, xl, c = row // 4, (row // 2) % 2, row % 2
    z, xh = aux // 2, aux % 2

    left_o, right_o = orbitals[:, :half], orbitals[:, half:]
    mine = jnp.where(c == 0, left_o, right_o)
    theirs = swap_cores(jnp.where(c == 0, right_o, left_o))
    f_own = factors[0]
    f_oth = swap_cores(after(f_own, theirs))
    first = jnp.where(c == 0, mine, theirs)
    second = jnp.where(c == 0, theirs, mine)
    piece = jnp.concatenate([first, second], axis=0)

    chip_rows = 2 * block_rows

    v = piece

    def at(yy, ll):
        return (yy % NY) * 2 + ll

    def turn(c, z):
        return (1 - 2 * c) * (1 - 2 * (z % 2))

    def along_y_turned(block):
        return move(block, lambda y, xl, c, z, xh: (y + turn(c, z), xl, c, z, xh))

    def swap_z(block):
        return move(block, lambda y, xl, c, z, xh: (y, xl, c, z + turn(c, z), xh))

    s = turn(c, z)
    a, x0 = lockstep(along_y_turned(v), along_x_by_core(v))
    b, x1, y2 = swap_z(a), along_x_by_core(a), along_y_turned(a)
    sofar = transform(f_own, f_oth, [v, x0, a], [at(y, xl), at(y, 1 - xl), at(y - s, xl)])
    b, x1, y2, sofar = lockstep(b, x1, y2, sofar)
    x2, y3 = along_x_by_core(b), along_y_turned(x1)
    sofar = transform(f_own, f_oth, [b, x1, y2], [at(y + s, xl), at(y - s, 1 - xl), at(y + 2, xl)], sofar)
    x2, y3, sofar = lockstep(x2, y3, sofar)
    both = transform(f_own, f_oth, [x2, y3], [at(y + s, 1 - xl), at(y + 2, 1 - xl)], sofar)
    keep_b, send_b = both[:block_rows], both[block_rows:]

    mine_q = jnp.where(xh == c, keep_b, send_b)
    rest_q = jnp.where(xh == c, send_b, keep_b)
    mine_n = flip_x(rest_q, 0, 1)
    b_own = jnp.concatenate([keep_b, swap_cores(send_b)], axis=1)
    mine_n, b_own = lockstep(mine_n, b_own)
    col0 = jnp.concatenate([mine_q, mine_n], axis=1)
    n1 = flip_x(b_own, 1, 0)
    n2 = flip_x(b_own, 1, 1)
    plus = along_y(col0, -1)
    minus = along_y(col0, 1)
    n1, n2, plus, minus = lockstep(n1, n2, plus, minus)
    far = along_y_by_core(jnp.where(c == 0, minus, plus), 1)
    n3 = move(jnp.where(c == 0, n2, n1), lambda y, xl, c, z, xh: (y, 1 - xl, c, z, xh if c == 0 else 1 - xh))

    q = half
    n = block_rows

    def right(own_half, other_half):
        pairs = [split(t[:, k * q:(k + 1) * q]) for k in (0, 1) for t in (own_half, other_half)]
        return jnp.concatenate([t for hi, lo in pairs for t in (hi, hi, lo)], axis=1)

    def left(own_q, other_q):
        pairs = [split(t[:, k * q:(k + 1) * q]) for t in (own_q, other_q) for k in (0, 1)]
        return jnp.concatenate([t for hi, lo in pairs for t in (hi, lo, hi)], axis=1)

    sub = block_rows // NZ
    near = jnp.concatenate([col0, plus, minus], axis=0)
    near = right(near, swap_cores(near))
    oth = left(n1, n2)
    k_oth = mm_t(oth, near).reshape(NZ, sub, 3 * n)
    far, n3, k_oth = lockstep(far, n3, k_oth)
    far = right(far, swap_cores(far))
    own = left(b_own, n3)
    k_own = mm_t(own, near).reshape(NZ, sub, 3 * n)
    k_far = mm_t(jnp.concatenate([own, oth], axis=0), far).reshape(2, NZ, sub, n)

    def part(d):
        def at_z(t):
            return lax.dynamic_index_in_dim(t, (z + d) % NZ, 0, keepdims=False)

        return jnp.concatenate([
            jnp.concatenate([at_z(k_own), at_z(k_far[0])], axis=1),
            jnp.concatenate([at_z(k_oth), at_z(k_far[1])], axis=1)], axis=0)

    g = reduce_z(part)

    out_rows = sub // 2

    def spread(own, oth):
        def pick(t, which):
            return lax.dynamic_index_in_dim(
                t.reshape(2, out_rows, t.shape[-1]), which, 0, keepdims=False)

        return [pick(own, xh), flip_x(pick(oth, xh), 1, 0), flip_x(pick(oth, 1 - xh), 1, 1),
                flip_x(pick(own, 1 - xh), 0, 1)]

    n = block_rows
    outs = []
    for e in spread(g[:sub], g[sub:]):
        rel = [e[:, :n], e[:, n:2 * n], e[:, 3 * n:], e[:, 2 * n:3 * n]]
        rel = jnp.stack(rel + rel[:3], axis=0)
        outs.append(lax.dynamic_slice_in_dim(rel, (NY - y) % NY, NY, 0))
    p0, p1, p2, p3 = outs
    q00 = jnp.where(xh == 0, p0, p3)
    q01 = jnp.where(xh == 0, p3, p0)
    q10 = jnp.where(xh == 0, p1, p2)
    q11 = jnp.where(xh == 0, p2, p1)
    lo = xl == 0
    blocks = [jnp.where(lo, q00, q10), jnp.where(lo, q01, q11), jnp.where(lo, q10, q00), jnp.where(lo, q11, q01)]
    pieces = [blocks[j][yy] for yy in range(NY) for j in range(4)]
    return jnp.concatenate(pieces, axis=1)


def solution(mesh):
    return jax.shard_map(
        shards,
        mesh=mesh,
        in_specs=(P("aux", "row", None), P("row", None)),
        out_specs=P(("row", "aux"), None),
        check_vma=False,
    )
```

```python
import functools

import jax
import jax.numpy as jnp
from jax import lax
from jax.experimental import pallas as pl
from jax.experimental.pallas import tpu as pltpu
from jax.sharding import PartitionSpec as P

AXES = ("row", "aux")
NY, NXL, NC, NZ, NXH = 4, 2, 2, 8, 2


def linear(y, xl, c, z, xh):
    row = ((y % NY) * NXL + xl) * NC + c
    return row * (NZ * NXH) + (z % NZ) * NXH + xh


def move(block, target):
    route = []
    for y in range(NY):
        for xl in range(NXL):
            for c in range(NC):
                for z in range(NZ):
                    for xh in range(NXH):
                        route.append((linear(y, xl, c, z, xh), linear(*target(y, xl, c, z, xh))))
    return lax.ppermute(block, AXES, route)


def swap_cores(b):
    return move(b, lambda y, xl, c, z, xh: (y, xl, 1 - c, z, xh))


def along_y(b, step):
    return move(b, lambda y, xl, c, z, xh: (y + step, xl, c, z, xh))


def along_z(b, step):
    return move(b, lambda y, xl, c, z, xh: (y, xl, c, z + step, xh))


def along_y_by_core(b, sign):
    return move(b, lambda y, xl, c, z, xh: (y + sign * (1 - 2 * c), xl, c, z, xh))


def along_x_by_core(b):
    def target(y, xl, c, z, xh):
        x = (xh * 2 + xl + (1 - 2 * c)) % 4
        return y, x % 2, c, z, x // 2

    return move(b, target)


def flip_x(b, flip_lo, flip_hi):
    return move(b, lambda y, xl, c, z, xh: (y, xl ^ flip_lo, c, z, xh ^ flip_hi))


def after(value, *earlier):
    return lax.optimization_barrier((value,) + earlier)[0]


def split(v):
    hi = lax.reduce_precision(v, 8, 7)
    return hi.astype(jnp.bfloat16), (v - hi).astype(jnp.bfloat16)


STEPS = 1


def halves(v):
    hi = v.astype(jnp.bfloat16)
    return hi, (v - hi.astype(jnp.float32)).astype(jnp.bfloat16)


def transform_kernel(count, has_acc, where_ref, own_ref, oth_ref, *refs):
    c_refs, rest = refs[:count], refs[count:]
    out_ref, ordered_refs = rest[has_acc], rest[has_acc + 1:]
    k = pl.program_id(0)

    @pl.when(k == 0)
    def _():
        out_ref[...] = rest[0][...] if has_acc else jnp.zeros_like(out_ref)

    rows, tile = own_ref.shape

    def one(c_ref):
        start = pl.multiple_of(lax.rem(k, STEPS) * tile, tile)
        c_hi, c_lo = halves(c_ref[pl.ds(start, tile), :])
        c_all = jnp.concatenate([c_hi, c_lo, c_hi], axis=0)
        for h, f_ref in enumerate((own_ref, oth_ref)):
            f_hi, f_lo = halves(f_ref[...])
            f_all = jnp.concatenate([f_hi, f_hi, f_lo], axis=1)
            out_ref[h * rows:(h + 1) * rows, :] += jnp.dot(f_all, c_all, preferred_element_type=jnp.float32)

    for p in range(count):
        pl.when(k // STEPS == p)(functools.partial(one, c_refs[p]))

    if ordered_refs:
        @pl.when(k == count * STEPS - 1)
        def _():
            first, second = out_ref[:rows, :], out_ref[rows:, :]
            keep_first = where_ref[count] == 1
            ordered_refs[0][...] = jnp.where(keep_first, first, second)
            ordered_refs[1][...] = jnp.where(keep_first, second, first)


def transform(f_own, f_oth, blocks, indices, acc=None, keep_first=None):
    rows = f_own.shape[0]
    depth, width = blocks[0].shape
    count = len(blocks)
    tile = depth // STEPS
    f_spec = pl.BlockSpec((rows, tile), lambda k, w: (0, w[k // STEPS] * STEPS + lax.rem(k, STEPS)))
    whole = pl.BlockSpec((2 * rows, width), lambda k, w: (0, 0))
    extra = [] if acc is None else [acc]
    out_specs, out_shape = whole, jax.ShapeDtypeStruct((2 * rows, width), jnp.float32)
    if keep_first is not None:
        indices = indices + [keep_first]
        out_specs = [whole] + [pl.BlockSpec((rows, width), lambda k, w: (0, 0))] * 2
        out_shape = [out_shape] + [jax.ShapeDtypeStruct((rows, width), jnp.float32)] * 2
    return pl.pallas_call(
        functools.partial(transform_kernel, count, len(extra)),
        grid_spec=pltpu.PrefetchScalarGridSpec(
            num_scalar_prefetch=1,
            grid=(count * STEPS,),
            in_specs=[f_spec, f_spec] + [whole] * (count + len(extra)),
            out_specs=out_specs,
        ),
        out_shape=out_shape,
        input_output_aliases={} if acc is None else {3 + count: 0},
        cost_estimate=pl.CostEstimate(
            flops=12 * count * rows * depth * width, bytes_accessed=12 * count * rows * depth, transcendentals=0),
        compiler_params=pltpu.CompilerParams(vmem_limit_bytes=56 * 1024 * 1024),
    )(jnp.stack([jnp.asarray(i, jnp.int32) for i in indices]), f_own, f_oth, *blocks, *extra)


def mm_t(a, b):
    return lax.dot_general(a, b, (((1,), (1,)), ((), ())), preferred_element_type=jnp.float32)


def lockstep(*values):
    return lax.optimization_barrier(values)


def outgoing(part, hop, up, down):
    if hop == 1:
        t = part(4)
        h = t.shape[0] // 2
        return t[:h], t[h:]
    if hop == 2:
        h = up.shape[0]
        p, m = part(3), part(5)
        return (jnp.concatenate([p[:h] + up, p[h:]], axis=0), jnp.concatenate([m[:h], m[h:] + down], axis=0))
    d = 5 - hop
    return up + part(d), down + part(8 - d)


def hop_z(sent):
    return along_z(sent[0], 1), along_z(sent[1], -1)


def shards(factors, orbitals):
    block_rows = factors.shape[1]
    occ = orbitals.shape[1]
    half = occ // 2
    row = lax.axis_index("row")
    aux = lax.axis_index("aux")
    y, xl, c = row // 4, (row // 2) % 2, row % 2
    z, xh = aux // 2, aux % 2

    left_o, right_o = orbitals[:, :half], orbitals[:, half:]
    mine = jnp.where(c == 0, left_o, right_o)
    theirs = swap_cores(jnp.where(c == 0, right_o, left_o))
    f_own = factors[0]
    f_oth = swap_cores(after(f_own, theirs))
    first = jnp.where(c == 0, mine, theirs)
    second = jnp.where(c == 0, theirs, mine)
    piece = jnp.concatenate([first, second], axis=0)

    chip_rows = 2 * block_rows

    width = half // 2
    n = block_rows
    sub = n // NZ

    def at(yy, ll):
        return (yy % NY) * 2 + ll

    def turn(c, z):
        return (1 - 2 * c) * (1 - 2 * (z % 2))

    def along_y_turned(block):
        return move(block, lambda y, xl, c, z, xh: (y + turn(c, z), xl, c, z, xh))

    def swap_z(block):
        return move(block, lambda y, xl, c, z, xh: (y, xl, c, z + turn(c, z), xh))

    s = turn(c, z)

    def hop1(v):
        return along_y_turned(v), along_x_by_core(v)

    def hop2(a, x0):
        return swap_z(a), along_x_by_core(a), along_y_turned(a)

    def sum1(v, a, x0):
        return transform(f_own, f_oth, [v, x0, a], [at(y, xl), at(y, 1 - xl), at(y - s, xl)])

    def hop3(b, x1):
        return along_x_by_core(b), along_y_turned(x1)

    def sum2(b, x1, y2, sofar):
        return transform(f_own, f_oth, [b, x1, y2], [at(y + s, xl), at(y - s, 1 - xl), at(y + 2, xl)], sofar)

    def sum3(x2, y3, sofar):
        return transform(
            f_own, f_oth, [x2, y3], [at(y + s, 1 - xl), at(y + 2, 1 - xl)], sofar, xh == c)

    def hop4(both, rest_q):
        return flip_x(rest_q, 0, 1), jnp.concatenate([both[:n], swap_cores(both[n:])], axis=1)

    def hop5(b_own, col0):
        return flip_x(b_own, 1, 0), flip_x(b_own, 1, 1), along_y(col0, -1), along_y(col0, 1)

    def hop6(n1, n2, plus, minus):
        far = along_y_by_core(jnp.where(c == 0, minus, plus), 1)
        n3 = move(jnp.where(c == 0, n2, n1), lambda y, xl, c, z, xh: (y, 1 - xl, c, z, xh if c == 0 else 1 - xh))
        return far, n3

    def right(own_half, other_half):
        pairs = [split(t[:, k * width:(k + 1) * width]) for k in (0, 1) for t in (own_half, other_half)]
        return jnp.concatenate([t for hi, lo in pairs for t in (hi, hi, lo)], axis=1)

    def left(own_q, other_q):
        pairs = [split(t[:, k * width:(k + 1) * width]) for t in (own_q, other_q) for k in (0, 1)]
        return jnp.concatenate([t for hi, lo in pairs for t in (hi, lo, hi)], axis=1)

    a, x0 = lockstep(*hop1(piece))
    b, x1, y2, sofar = lockstep(*hop2(a, x0), sum1(piece, a, x0))
    x2, y3, sofar = lockstep(*hop3(b, x1), sum2(b, x1, y2, sofar))
    both, mine, rest = sum3(x2, y3, sofar)
    both0, both1 = both[:, :width], both[:, width:]
    mine0, mine1 = mine[:, :width], mine[:, width:]
    rest0, rest1 = rest[:, :width], rest[:, width:]
    got4 = hop4(both0, rest0)
    got4_1 = hop4(both1, rest1)
    mine_n0, b_own0, _ = lockstep(*got4, rest1)
    col0 = jnp.concatenate([mine0, mine_n0], axis=1)
    got5 = hop5(b_own0, col0)
    mine_n1, b_own1, _ = lockstep(*got4_1, col0)
    col1 = jnp.concatenate([mine1, mine_n1], axis=1)
    got5_1 = hop5(b_own1, col1)
    n1, n2, plus, minus, _ = lockstep(*got5, col1)
    far0, n30 = hop6(n1, n2, plus, minus)
    near0 = jnp.concatenate([col0, plus, minus], axis=0)
    near0 = right(near0, swap_cores(near0))
    oth0 = left(n1, n2)
    k_oth0 = mm_t(oth0, near0)
    n1, n2, plus, minus, _ = lockstep(*got5_1, k_oth0)
    far1, n31 = hop6(n1, n2, plus, minus)
    near1 = jnp.concatenate([col1, plus, minus], axis=0)
    near1 = right(near1, swap_cores(near1))
    oth1 = left(n1, n2)
    far0, n30, near1 = lockstep(far0, n30, near1)
    own0 = left(b_own0, n30)
    far0 = right(far0, swap_cores(far0))
    k_oth = k_oth0 + mm_t(oth1, near1)
    k_own0 = mm_t(own0, near0)
    k_far0 = mm_t(jnp.concatenate([own0, oth0], axis=0), far0)
    far1, n31, k_oth, k_own0, k_far0 = lockstep(far1, n31, k_oth, k_own0, k_far0)
    own1 = left(b_own1, n31)
    k_own = k_own0 + mm_t(own1, near1)
    far1 = right(far1, swap_cores(far1))
    far1, k_own = lockstep(far1, k_own)
    k_oth_far = (k_far0[n:] + mm_t(oth1, far1)).reshape(NZ, sub, n)
    k_own_far = (k_far0[:n] + mm_t(own1, far1)).reshape(NZ, sub, n)
    k_own, k_oth = k_own.reshape(NZ, sub, 3 * n), k_oth.reshape(NZ, sub, 3 * n)

    def part_of(k_near, k_far):
        def part(d):
            return jnp.concatenate(
                [lax.dynamic_index_in_dim(t, (z + d) % NZ, 0, keepdims=False) for t in (k_near, k_far)], axis=1)

        return part

    part_b = part_of(k_oth, k_oth_far)
    sent_b = outgoing(part_b, 1, None, None)
    got_b = hop_z(sent_b)
    part_a = part_of(k_own, k_own_far)
    sent_a = outgoing(part_a, 1, None, None)
    got_a = hop_z(sent_a)
    for hop in (2, 3, 4):
        up, down, *_ = lockstep(*got_b, *sent_a)
        sent_b = outgoing(part_b, hop, up, down)
        got_b = hop_z(sent_b)
        up, down, *_ = lockstep(*got_a, *sent_b)
        sent_a = outgoing(part_a, hop, up, down)
        got_a = hop_z(sent_a)
    up, down, *_ = lockstep(*got_b, *sent_a)
    g_oth = up + down + part_b(0)

    out_rows = sub // 2

    def pick(t, which):
        return lax.dynamic_index_in_dim(t.reshape(2, out_rows, t.shape[-1]), which, 0, keepdims=False)

    to_1, to_2 = pick(g_oth, xh), pick(g_oth, 1 - xh)
    up, down, *_ = lockstep(*got_a, to_1, to_2)
    g_own = up + down + part_a(0)
    spread = [pick(g_own, xh), flip_x(to_1, 1, 0), flip_x(to_2, 1, 1), flip_x(pick(g_own, 1 - xh), 0, 1)]
    outs = []
    for e in spread:
        rel = [e[:, :n], e[:, n:2 * n], e[:, 3 * n:], e[:, 2 * n:3 * n]]
        rel = jnp.stack(rel + rel[:3], axis=0)
        outs.append(lax.dynamic_slice_in_dim(rel, (NY - y) % NY, NY, 0))
    p0, p1, p2, p3 = outs
    q00 = jnp.where(xh == 0, p0, p3)
    q01 = jnp.where(xh == 0, p3, p0)
    q10 = jnp.where(xh == 0, p1, p2)
    q11 = jnp.where(xh == 0, p2, p1)
    lo = xl == 0
    blocks = [jnp.where(lo, q00, q10), jnp.where(lo, q01, q11), jnp.where(lo, q10, q00), jnp.where(lo, q11, q01)]
    pieces = [blocks[j][yy] for yy in range(NY) for j in range(4)]
    return jnp.concatenate(pieces, axis=1)


def solution(mesh):
    return jax.shard_map(
        shards,
        mesh=mesh,
        in_specs=(P("aux", "row", None), P("row", None)),
        out_specs=P(("row", "aux"), None),
        check_vma=False,
    )
```

```python
import functools

import jax
import jax.numpy as jnp
from jax import lax
from jax.experimental import pallas as pl
from jax.experimental.pallas import tpu as pltpu
from jax.sharding import PartitionSpec as P

AXES = ("row", "aux")
NY, NXL, NC, NZ, NXH = 4, 2, 2, 8, 2


def linear(y, xl, c, z, xh):
    row = ((y % NY) * NXL + xl) * NC + c
    return row * (NZ * NXH) + (z % NZ) * NXH + xh


def move(block, target):
    route = []
    for y in range(NY):
        for xl in range(NXL):
            for c in range(NC):
                for z in range(NZ):
                    for xh in range(NXH):
                        route.append((linear(y, xl, c, z, xh), linear(*target(y, xl, c, z, xh))))
    return lax.ppermute(block, AXES, route)


def swap_cores(b):
    return move(b, lambda y, xl, c, z, xh: (y, xl, 1 - c, z, xh))


def along_y(b, step):
    return move(b, lambda y, xl, c, z, xh: (y + step, xl, c, z, xh))


def along_z(b, step):
    return move(b, lambda y, xl, c, z, xh: (y, xl, c, z + step, xh))


def along_y_by_core(b, sign):
    return move(b, lambda y, xl, c, z, xh: (y + sign * (1 - 2 * c), xl, c, z, xh))


def along_x_by_core(b):
    def target(y, xl, c, z, xh):
        x = (xh * 2 + xl + (1 - 2 * c)) % 4
        return y, x % 2, c, z, x // 2

    return move(b, target)


def flip_x(b, flip_lo, flip_hi):
    return move(b, lambda y, xl, c, z, xh: (y, xl ^ flip_lo, c, z, xh ^ flip_hi))


def after(value, *earlier):
    return lax.optimization_barrier((value,) + earlier)[0]


def split(v):
    hi = lax.reduce_precision(v, 8, 7)
    return hi.astype(jnp.bfloat16), (v - hi).astype(jnp.bfloat16)


CORE, KEEP_FIRST = 8, 9


def halves(v):
    hi = v.astype(jnp.bfloat16)
    return hi, (v - hi.astype(jnp.float32)).astype(jnp.bfloat16)


def transform_kernel(count, has_acc, where_ref, own_ref, oth_ref, *refs):
    c_refs, rest = refs[:2 * count], refs[2 * count:]
    out_ref, last_refs = rest[has_acc], rest[has_acc + 1:]
    k = pl.program_id(0)

    @pl.when(k == 0)
    def _():
        out_ref[...] = rest[0][...] if has_acc else jnp.zeros_like(out_ref)

    rows = own_ref.shape[0]
    core = where_ref[CORE]

    def one(*parts):
        v = jnp.concatenate([
            jnp.concatenate([ref[pl.ds(pl.multiple_of(place * rows, rows), rows), :] for ref in parts], axis=1)
            for place in (core, 1 - core)], axis=0)
        c_hi, c_lo = halves(v)
        c_all = jnp.concatenate([c_hi, c_lo, c_hi], axis=0)
        for h, f_ref in enumerate((own_ref, oth_ref)):
            f_hi, f_lo = halves(f_ref[...])
            f_all = jnp.concatenate([f_hi, f_hi, f_lo], axis=1)
            out_ref[h * rows:(h + 1) * rows, :] += jnp.dot(f_all, c_all, preferred_element_type=jnp.float32)

    for p in range(count):
        pl.when(k == p)(functools.partial(one, *c_refs[2 * p:2 * p + 2]))

    if last_refs:
        @pl.when(k == count - 1)
        def _():
            first, second = out_ref[:rows, :], out_ref[rows:, :]
            keep_first = where_ref[KEEP_FIRST] == 1
            mine, rest_rows = jnp.where(keep_first, first, second), jnp.where(keep_first, second, first)
            width = last_refs[0].shape[1]
            for place, t in enumerate((first, second, mine, rest_rows)):
                last_refs[2 * place][...] = t[:, :width]
                last_refs[2 * place + 1][...] = t[:, width:]


def transform(f_own, f_oth, where, base, blocks, acc=None, last=False):
    rows = f_own.shape[0]
    depth, width = blocks[0][0].shape
    count = len(blocks)
    f_spec = pl.BlockSpec((rows, depth), lambda k, w: (0, w[base + k]))
    whole = pl.BlockSpec((2 * rows, 2 * width), lambda k, w: (0, 0))
    part = pl.BlockSpec((depth, width), lambda k, w: (0, 0))
    extra = [] if acc is None else [acc]
    out_specs, out_shape = whole, jax.ShapeDtypeStruct((2 * rows, 2 * width), jnp.float32)
    if last:
        out_specs = [whole] + [pl.BlockSpec((rows, width), lambda k, w: (0, 0))] * 8
        out_shape = [out_shape] + [jax.ShapeDtypeStruct((rows, width), jnp.float32)] * 8
    return pl.pallas_call(
        functools.partial(transform_kernel, count, len(extra)),
        grid_spec=pltpu.PrefetchScalarGridSpec(
            num_scalar_prefetch=1,
            grid=(count,),
            in_specs=[f_spec, f_spec] + [part] * (2 * count) + [whole] * len(extra),
            out_specs=out_specs,
        ),
        out_shape=out_shape,
        input_output_aliases={} if acc is None else {3 + 2 * count: 0},
        cost_estimate=pl.CostEstimate(
            flops=24 * count * rows * depth * width, bytes_accessed=12 * count * rows * depth, transcendentals=0),
        compiler_params=pltpu.CompilerParams(vmem_limit_bytes=56 * 1024 * 1024),
    )(where, f_own, f_oth, *(half for block in blocks for half in block), *extra)


def mm_t(a, b):
    return lax.dot_general(a, b, (((1,), (1,)), ((), ())), preferred_element_type=jnp.float32)


def lockstep(*values):
    return lax.optimization_barrier(values)


def outgoing(part, hop, up, down):
    if hop == 1:
        t = part(4)
        h = t.shape[0] // 2
        return t[:h], t[h:]
    if hop == 2:
        h = up.shape[0]
        p, m = part(3), part(5)
        return (jnp.concatenate([p[:h] + up, p[h:]], axis=0), jnp.concatenate([m[:h], m[h:] + down], axis=0))
    d = 5 - hop
    return up + part(d), down + part(8 - d)


def hop_z(sent):
    return along_z(sent[0], 1), along_z(sent[1], -1)


def shards(factors, orbitals):
    block_rows = factors.shape[1]
    occ = orbitals.shape[1]
    half = occ // 2
    row = lax.axis_index("row")
    aux = lax.axis_index("aux")
    y, xl, c = row // 4, (row // 2) % 2, row % 2
    z, xh = aux // 2, aux % 2

    left_o, right_o = orbitals[:, :half], orbitals[:, half:]
    mine = jnp.where(c == 0, left_o, right_o)
    theirs = swap_cores(jnp.where(c == 0, right_o, left_o))
    f_own = factors[0]
    f_oth = swap_cores(after(f_own, theirs))
    piece = jnp.concatenate([mine, theirs], axis=0)

    width = half // 2
    n = block_rows
    sub = n // NZ

    def at(yy, ll):
        return (yy % NY) * 2 + ll

    def turn(c, z):
        return (1 - 2 * c) * (1 - 2 * (z % 2))

    def along_y_turned(block):
        return move(block, lambda y, xl, c, z, xh: (y + turn(c, z), xl, c, z, xh))

    def swap_z(block):
        return move(block, lambda y, xl, c, z, xh: (y, xl, c, z + turn(c, z), xh))

    s = turn(c, z)

    where = jnp.stack([jnp.asarray(t, jnp.int32) for t in (
        at(y, xl), at(y - s, xl), at(y, 1 - xl), at(y + s, xl), at(y - s, 1 - xl), at(y + 2, xl),
        at(y + s, 1 - xl), at(y + 2, 1 - xl), c, xh == c)])

    def hop1(v):
        return along_y_turned(v), along_x_by_core(v)

    def hop2(a, x0):
        return swap_z(a), along_x_by_core(a), along_y_turned(a)

    def hop3(b, x1):
        return along_x_by_core(b), along_y_turned(x1)

    def hop4(keep, send, rest_q):
        return flip_x(rest_q, 0, 1), jnp.concatenate([keep, swap_cores(send)], axis=1)

    def hop5(b_own, col0):
        return flip_x(b_own, 1, 0), flip_x(b_own, 1, 1), along_y(col0, -1), along_y(col0, 1)

    def hop6(n1, n2, plus, minus):
        far = along_y_by_core(jnp.where(c == 0, minus, plus), 1)
        n3 = move(jnp.where(c == 0, n2, n1), lambda y, xl, c, z, xh: (y, 1 - xl, c, z, xh if c == 0 else 1 - xh))
        return far, n3

    def right(own_half, other_half):
        pairs = [split(t[:, k * width:(k + 1) * width]) for k in (0, 1) for t in (own_half, other_half)]
        return jnp.concatenate([t for hi, lo in pairs for t in (hi, hi, lo)], axis=1)

    def left(own_q, other_q):
        pairs = [split(t[:, k * width:(k + 1) * width]) for t in (own_q, other_q) for k in (0, 1)]
        return jnp.concatenate([t for hi, lo in pairs for t in (hi, lo, hi)], axis=1)

    v0, v1 = piece[:, :width], piece[:, width:]
    got_0, got_1 = hop1(v0), hop1(v1)
    a0, x00 = lockstep(*got_0)
    got_0 = hop2(a0, x00)
    a1, x01, _ = lockstep(*got_1, a0)
    got_1 = hop2(a1, x01)
    sofar = transform(f_own, f_oth, where, 0, [(v0, v1), (a0, a1), (x00, x01)])
    b0, x10, y20, sofar = lockstep(*got_0, sofar)
    got_0 = hop3(b0, x10)
    b1, x11, y21, _ = lockstep(*got_1, x10)
    got_1 = hop3(b1, x11)
    sofar = transform(f_own, f_oth, where, 3, [(b0, b1), (x10, x11), (y20, y21)], sofar)
    x20, y30, x21, y31, sofar = lockstep(*got_0, *got_1, sofar)
    _, keep0, keep1, send0, send1, mine0, mine1, rest0, rest1 = transform(
        f_own, f_oth, where, 6, [(x20, x21), (y30, y31)], sofar, True)
    got4 = hop4(keep0, send0, rest0)
    got4_1 = hop4(keep1, send1, rest1)
    mine_n0, b_own0, _ = lockstep(*got4, rest1)
    col0 = jnp.concatenate([mine0, mine_n0], axis=1)
    got5 = hop5(b_own0, col0)
    mine_n1, b_own1, _ = lockstep(*got4_1, col0)
    col1 = jnp.concatenate([mine1, mine_n1], axis=1)
    got5_1 = hop5(b_own1, col1)
    n1, n2, plus, minus, _ = lockstep(*got5, col1)
    far0, n30 = hop6(n1, n2, plus, minus)
    near0 = jnp.concatenate([col0, plus, minus], axis=0)
    near0 = right(near0, swap_cores(near0))
    oth0 = left(n1, n2)
    k_oth0 = mm_t(oth0, near0)
    n1, n2, plus, minus, _ = lockstep(*got5_1, k_oth0)
    far1, n31 = hop6(n1, n2, plus, minus)
    near1 = jnp.concatenate([col1, plus, minus], axis=0)
    near1 = right(near1, swap_cores(near1))
    oth1 = left(n1, n2)
    far0, n30, near1 = lockstep(far0, n30, near1)
    own0 = left(b_own0, n30)
    far0 = right(far0, swap_cores(far0))
    k_oth = k_oth0 + mm_t(oth1, near1)
    k_own0 = mm_t(own0, near0)
    k_far0 = mm_t(jnp.concatenate([own0, oth0], axis=0), far0)
    far1, n31, k_oth, k_own0, k_far0 = lockstep(far1, n31, k_oth, k_own0, k_far0)
    own1 = left(b_own1, n31)
    k_own = k_own0 + mm_t(own1, near1)
    far1 = right(far1, swap_cores(far1))
    far1, k_own = lockstep(far1, k_own)
    k_oth_far = (k_far0[n:] + mm_t(oth1, far1)).reshape(NZ, sub, n)
    k_own_far = (k_far0[:n] + mm_t(own1, far1)).reshape(NZ, sub, n)
    k_own, k_oth = k_own.reshape(NZ, sub, 3 * n), k_oth.reshape(NZ, sub, 3 * n)

    def part_of(k_near, k_far):
        def part(d):
            return jnp.concatenate(
                [lax.dynamic_index_in_dim(t, (z + d) % NZ, 0, keepdims=False) for t in (k_near, k_far)], axis=1)

        return part

    part_b = part_of(k_oth, k_oth_far)
    sent_b = outgoing(part_b, 1, None, None)
    got_b = hop_z(sent_b)
    part_a = part_of(k_own, k_own_far)
    sent_a = outgoing(part_a, 1, None, None)
    got_a = hop_z(sent_a)
    for hop in (2, 3, 4):
        up, down, *_ = lockstep(*got_b, *sent_a)
        sent_b = outgoing(part_b, hop, up, down)
        got_b = hop_z(sent_b)
        up, down, *_ = lockstep(*got_a, *sent_b)
        sent_a = outgoing(part_a, hop, up, down)
        got_a = hop_z(sent_a)
    up, down, *_ = lockstep(*got_b, *sent_a)
    g_oth = up + down + part_b(0)

    out_rows = sub // 2

    def pick(t, which):
        return lax.dynamic_index_in_dim(t.reshape(2, out_rows, t.shape[-1]), which, 0, keepdims=False)

    to_1, to_2 = pick(g_oth, xh), pick(g_oth, 1 - xh)
    up, down, *_ = lockstep(*got_a, to_1, to_2)
    g_own = up + down + part_a(0)
    spread = [pick(g_own, xh), flip_x(to_1, 1, 0), flip_x(to_2, 1, 1), flip_x(pick(g_own, 1 - xh), 0, 1)]
    outs = []
    for e in spread:
        rel = [e[:, :n], e[:, n:2 * n], e[:, 3 * n:], e[:, 2 * n:3 * n]]
        rel = jnp.stack(rel + rel[:3], axis=0)
        outs.append(lax.dynamic_slice_in_dim(rel, (NY - y) % NY, NY, 0))
    p0, p1, p2, p3 = outs
    q00 = jnp.where(xh == 0, p0, p3)
    q01 = jnp.where(xh == 0, p3, p0)
    q10 = jnp.where(xh == 0, p1, p2)
    q11 = jnp.where(xh == 0, p2, p1)
    lo = xl == 0
    blocks = [jnp.where(lo, q00, q10), jnp.where(lo, q01, q11), jnp.where(lo, q10, q00), jnp.where(lo, q11, q01)]
    pieces = [blocks[j][yy] for yy in range(NY) for j in range(4)]
    return jnp.concatenate(pieces, axis=1)


def solution(mesh):
    return jax.shard_map(
        shards,
        mesh=mesh,
        in_specs=(P("aux", "row", None), P("row", None)),
        out_specs=P(("row", "aux"), None),
        check_vma=False,
    )
```
